32 devices in a mesh: groups: 2 (over x), expert: 8 (over z, y), dp: 2 (over core).
Axes of the slice: x: 2, y: 2, z: 4, core: 2. Of those that a mesh axis runs over, the one named last changes fastest.
Arguments:
- tokens: bfloat16 [1280, 4096], P(('groups', 'expert', 'dp')), parts along dimension 0, may hold values from -25 to 25
- routing: int32 [1280, 8], P(('groups', 'expert', 'dp')), parts along dimension 0, may hold values from 0 to 31, all different within a row; in each aligned block of 40 rows (0 to 39, 40 to 79, ...) at most 20 rows name the same one
- gate_weight: bfloat16 [32, 4096, 768], P('expert', 'dp'), may hold values from -0.09375 to 0.09375
- up_weight: bfloat16 [32, 4096, 768], P('expert', 'dp'), may hold values from -0.09375 to 0.09375
Outputs:
- input_gram: bfloat16 [2048, 64, 2048], P('dp', ('groups', 'expert')), parts along dimension 1
- hidden_gram: bfloat16 [768, 64, 768], P('dp', ('groups', 'expert')), parts along dimension 1
The draws below stay inside these ranges and needn't reach their ends.
There are 2 independent parts, one for each index of `groups`. The reference program is written for one: setup_inputs(seed, part) draws one part's arguments, and reference() takes and returns one part's arrays. A program takes and returns all parts, laid end to end along the dimension named above; an argument that names none is the same for every part. Nothing has to cross between parts.
Inputs may be any that keep to these rules, and one draw needn't show every extreme that they name: `routing`: each row names 8 different experts. Among the rows of one device no expert is named by more than 20 rows.
All inputs are finite; a program needn't handle non-finite values.
Results may differ from the reference program's by a relative error of at most 0.01.
Values may be sent and summed in bfloat16 or wider, within the bound.
A program may use at most 256 MiB of HBM per device.

```python
import math
import jax
import jax.numpy as jnp
import numpy as np
from jax import lax

D = 4096
DW = 2048
HW = 768
EXPERTS = 32
TOPK = 8
TOK_DEV = 40
CAP = 20
TOKENS = 640
N_EXPERT = 8
N_DP = 2


def draw_tokens(key, part):
    key = jax.random.fold_in(key, 11)
    channel_key, token_key, value_key = jax.random.split(key, 3)
    channel_scale = jnp.exp(jax.random.uniform(channel_key, (1, D), jnp.float32, math.log(0.5), math.log(3.0)))
    token_scale = jnp.exp(jax.random.uniform(token_key, (TOKENS, 1), jnp.float32, math.log(0.5), math.log(2.0)))
    values = jax.random.truncated_normal(value_key, -4.0, 4.0, (TOKENS, D), jnp.float32)
    return (values * channel_scale * token_scale).astype(jnp.bfloat16)


def steps_of(stream_key, extent, cuts, least, largest):
    def one(position, shards_of):
        steps = jax.random.uniform(jax.random.fold_in(jax.random.fold_in(stream_key, 6), position), (shards_of,), jnp.float32, least / len(cuts), largest / len(cuts))
        return jnp.repeat(jnp.exp(steps), extent[position] // shards_of).reshape((-1,) + (1,) * (len(extent) - position - 1))

    gain = one(*cuts[0])
    for cut in cuts[1:]:
        gain = gain * one(*cut)
    return gain


def deal_out(key, own, number, rows, amount, top, bound, slope):
    ranking = jax.random.permutation(key, amount)
    packed, common = shares(amount, rows * top, bound, slope, True), shares(amount, rows * top, bound, slope, False)
    places = jnp.arange(amount)

    def named(tallies, offset_by):
        used = int((tallies > 0).sum())
        fixed = max(1, used // 4)
        passed = fixed + (places - fixed + offset_by * (used - fixed)) % max(1, amount - fixed)
        return jnp.zeros((amount,), jnp.int32).at[ranking[jnp.where(places < fixed, places, passed)]].set(jnp.asarray(tallies, jnp.int32))

    tallies = jnp.where(number % 4 == 0, named(packed, number // 4), named(common, number - number // 4 - 1))
    mixed = jax.random.permutation(jax.random.fold_in(own, 3), amount)
    source_of, receiver = mixed[0:amount // 2 * 2:2], mixed[1:amount // 2 * 2:2]
    slack = jnp.minimum(tallies[source_of] - 1, bound - tallies[receiver]) // 2
    slack = jnp.where((source_of == ranking[0]) | (receiver == ranking[0]) | (tallies[receiver] == 0), 0, jnp.maximum(slack, 0))
    passed = jax.random.randint(jax.random.fold_in(own, 4), (amount // 2,), 0, 1 << 20) % (slack + 1)
    tallies = tallies.at[source_of].add(-passed).at[receiver].add(passed)
    members = jnp.searchsorted(jnp.cumsum(tallies), jnp.arange(rows * top), side="right").astype(jnp.int32)
    grid = members.reshape(top, rows).T
    grid = grid[jax.random.permutation(jax.random.fold_in(own, 1), rows)]
    offset_by = jax.random.randint(jax.random.fold_in(own, 2), (rows, 1), 0, top)
    return jnp.take_along_axis(grid, (jnp.arange(top)[None, :] + offset_by) % top, axis=1)


def shares(number_of, total, most, slope, full):
    portions = [(1 << 20) // math.isqrt(grade ** slope) + 1 for grade in range(1, number_of + 1)]
    largest = most if full else min(most, max(-(-total // number_of), total * portions[0] // sum(portions)))
    least = 1 if total - largest >= number_of - 1 else 0
    counts, surplus = [largest] + [least] * (number_of - 1), total - largest - least * (number_of - 1)
    while surplus > 0:
        free = [i for i in range(1, number_of) if counts[i] < largest] or [i for i in range(1, number_of) if counts[i] < most]
        pool, left = sum([portions[i] for i in free]), surplus
        for i in free:
            more = min(most - counts[i], max(1, left * portions[i] // pool), surplus)
            counts[i] = counts[i] + more
            surplus = surplus - more
    return np.array(counts)


def bell_draw(key, shape, scale, most, cuts=(), held_as=jnp.bfloat16):
    drawn = jax.random.normal(key, shape, jnp.float32) * scale
    if len(cuts) > 0:
        drawn = steps_of(key, shape, cuts, -0.22, 0.18) * drawn
    return jnp.clip(drawn, min=-most, max=most).astype(held_as)


def setup_inputs(seed: int = 0, part: int = 0) -> dict:
    key_list = jax.random.split(jax.random.key(seed), 5)
    part_keys = jax.random.split(jax.random.fold_in(key_list[4], part), 5)
    tokens = draw_tokens(jax.random.fold_in(jax.random.fold_in(key_list[4], part), 71), part)
    routing_keys = jax.random.split(jax.random.fold_in(part_keys[1], 1), TOKENS // TOK_DEV)
    routing_turns = jax.random.permutation(jax.random.fold_in(part_keys[1], 3), TOKENS // TOK_DEV)
    routing = jax.vmap(lambda own, number: deal_out(jax.random.fold_in(part_keys[1], 2), own, number, TOK_DEV, EXPERTS, TOPK, CAP, 2))(routing_keys, routing_turns).reshape((TOKENS, TOPK))
    gate_weight = bell_draw(key_list[2], (EXPERTS, D, HW), D ** -0.5, 0.09375, ((0, 8), (1, 2)))
    up_weight = bell_draw(key_list[3], (EXPERTS, D, HW), D ** -0.5, 0.09375, ((0, 8), (1, 2)))
    return dict(tokens=tokens, routing=routing, gate_weight=gate_weight, up_weight=up_weight)


def reference(tokens, routing, gate_weight, up_weight):
    factor = 2.0 / TOKENS
    most_rows = N_EXPERT * CAP
    positions = jnp.arange(TOKENS, dtype=jnp.int32)
    replica_of = (positions // TOK_DEV) % N_DP
    labels = jnp.arange(EXPERTS, dtype=jnp.int32)
    chosen = jnp.any(routing[:, :, None] == labels[None, None, :], axis=1)

    def per_expert(expert):
        input_total = jnp.zeros((DW, DW), jnp.float32)
        hidden_total = jnp.zeros((HW, HW), jnp.float32)
        for replica in range(N_DP):
            is_live = chosen[:, expert] & (replica_of == replica)
            sort_key = jnp.where(is_live, positions, positions + TOKENS)
            picked = jnp.argsort(sort_key)[:most_rows].astype(jnp.int32)
            present = is_live[picked].astype(jnp.bfloat16)
            routed = tokens[picked] * present[:, None]
            window = routed[:, :DW]
            input_part = jnp.dot(window.T, window, preferred_element_type=jnp.float32)
            gate_sum = jnp.dot(routed, gate_weight[expert], preferred_element_type=jnp.float32)
            up_sum = jnp.dot(routed, up_weight[expert], preferred_element_type=jnp.float32)
            hidden = (jax.nn.silu(gate_sum) * up_sum).astype(jnp.bfloat16)
            hidden_part = jnp.dot(hidden.T, hidden, preferred_element_type=jnp.float32)
            input_total = input_total + input_part.astype(jnp.bfloat16).astype(jnp.float32)
            hidden_total = hidden_total + hidden_part.astype(jnp.bfloat16).astype(jnp.float32)
        return (input_total * factor).astype(jnp.bfloat16), (hidden_total * factor).astype(jnp.bfloat16)

    input_all, hidden_all = lax.map(per_expert, labels)
    return jnp.transpose(input_all, (1, 0, 2)), jnp.transpose(hidden_all, (1, 0, 2))
```

```python
import jax
import jax.numpy as jnp
from jax import lax
from jax.sharding import PartitionSpec as P

DW = 2048


def local(tokens, routing, gate_weight, up_weight):
    expert_count = lax.axis_size("expert")
    replica_count = lax.axis_size("dp")
    core = lax.axis_index("dp")
    device_tokens, topk = routing.shape
    local_experts, depth, hidden_width = gate_weight.shape
    factor = 2.0 / (device_tokens * expert_count * replica_count)
    swap = [(0, 1), (1, 0)]

    names = jnp.pad(routing.astype(jnp.bfloat16), ((0, 0), (0, 128 - topk)))
    own_cols = lax.dynamic_slice_in_dim(tokens, core * depth, depth, 1)
    other_cols = lax.dynamic_slice_in_dim(tokens, (1 - core) * depth, depth, 1)
    own_rows = jnp.concatenate([own_cols, names], axis=1)
    other_rows = lax.ppermute(jnp.concatenate([other_cols, names], axis=1), "dp", swap)

    labels = lax.axis_index("expert") * local_experts + jnp.arange(local_experts)

    def gathered(rows):
        got = lax.all_gather(rows, "expert", axis=0, tiled=True)
        x = got[:, :depth]
        named = got[:, depth : depth + topk].astype(jnp.int32)
        mask = jnp.any(named[None, :, :] == labels[:, None, None], axis=2)
        return x, mask, lax.ppermute(x[:, :DW], "dp", [(0, 1)])

    own_x, own_mask, sent_own = gathered(own_rows)
    other_x, other_mask, sent_other = gathered(other_rows)
    own_window = jnp.where(core == 0, own_x[:, :DW], sent_other)
    other_window = jnp.where(core == 0, other_x[:, :DW], sent_own)

    def project(x, w):
        return jnp.einsum("td,edh->eth", x, w, preferred_element_type=jnp.float32)

    other_gate = lax.ppermute(project(other_x, gate_weight).astype(jnp.bfloat16), "dp", swap)
    other_up = lax.ppermute(project(other_x, up_weight).astype(jnp.bfloat16), "dp", swap)
    gate = project(own_x, gate_weight) + other_gate.astype(jnp.float32)
    up = project(own_x, up_weight) + other_up.astype(jnp.float32)
    hidden = jnp.where(own_mask[:, :, None], jax.nn.silu(gate) * up, 0.0).astype(jnp.bfloat16)
    other_hidden = lax.ppermute(hidden, "dp", swap)

    window = jnp.concatenate([own_window, other_window], axis=0)
    mask = jnp.concatenate([own_mask, other_mask], axis=1)
    block = DW // replica_count
    rows = lax.dynamic_slice_in_dim(window, core * block, block, 1).T
    left = jnp.where(mask[None, :, :], rows[:, None, :], jnp.bfloat16(0))
    input_gram = jnp.einsum("iet,tj->iej", left, window, preferred_element_type=jnp.float32)

    hidden_all = jnp.concatenate([hidden, other_hidden], axis=1)
    h_block = hidden_width // replica_count
    h_rows = lax.dynamic_slice_in_dim(hidden_all, core * h_block, h_block, 2)
    hidden_gram = jnp.einsum("eti,etj->iej", h_rows, hidden_all, preferred_element_type=jnp.float32)
    return ((input_gram * factor).astype(jnp.bfloat16), (hidden_gram * factor).astype(jnp.bfloat16))


def solution(mesh):
    placed = (
        P(("groups", "expert", "dp"), None),
        P(("groups", "expert", "dp"), None),
        P("expert", "dp", None),
        P("expert", "dp", None),
    )
    return jax.shard_map(
        local,
        mesh=mesh,
        in_specs=placed,
        out_specs=(P("dp", ("groups", "expert"), None), P("dp", ("groups", "expert"), None)),
        check_vma=False,
    )
```

```python
import functools

import jax
import jax.numpy as jnp
from jax import lax
from jax.experimental import pallas as pl
from jax.experimental.pallas import tpu as pltpu
from jax.sharding import PartitionSpec as P

DW = 2048
ROW_PAD = 16
MESH = pl.DeviceIdType.MESH


def gather_kernel(experts, cores, rows_ref, out_ref, send_sem, recv_sem, own_sem):
    expert, core = lax.axis_index("expert"), lax.axis_index("dp")
    number = experts * cores
    me = expert * cores + core

    def peer(step):
        index = lax.rem(me + step, number)
        return {"expert": index // cores, "dp": lax.rem(index, cores)}

    barrier = pltpu.get_barrier_semaphore()
    for step in range(1, number):
        pl.semaphore_signal(barrier, inc=1, device_id=peer(step), device_id_type=MESH)
    pl.semaphore_wait(barrier, number - 1)
    copies = []
    for step in range(1, number):
        target = peer(step)
        copy = pltpu.make_async_remote_copy(
            src_ref=rows_ref.at[target["dp"]],
            dst_ref=out_ref.at[lax.rem(core + target["dp"], cores), expert],
            send_sem=send_sem.at[step],
            recv_sem=recv_sem.at[step],
            device_id=target,
            device_id_type=MESH,
        )
        copy.start()
        copies.append(copy)
    own = pltpu.make_async_copy(rows_ref.at[core], out_ref.at[0, expert], own_sem)
    own.start()
    own.wait()
    for copy in copies:
        copy.wait()


def gather(rows, experts):
    cores = rows.shape[0]
    number = experts * cores
    return pl.pallas_call(
        functools.partial(gather_kernel, experts, cores),
        out_shape=jax.ShapeDtypeStruct((cores, experts) + rows.shape[1:], rows.dtype),
        in_specs=[pl.BlockSpec(memory_space=pl.ANY)],
        out_specs=pl.BlockSpec(memory_space=pl.ANY),
        scratch_shapes=[
            pltpu.SemaphoreType.DMA((number,)),
            pltpu.SemaphoreType.DMA((number,)),
            pltpu.SemaphoreType.DMA,
        ],
        compiler_params=pltpu.CompilerParams(collective_id=0, has_side_effects=True),
    )(rows)


def gram_kernel(factor, left_ref, right_ref, out_ref):
    total = jnp.dot(left_ref[...], right_ref[...], preferred_element_type=jnp.float32)
    out_ref[...] = (total * factor).reshape(out_ref.shape).astype(out_ref.dtype)


def gram(left, right, experts, factor):
    rows, depth = left.shape
    width = right.shape[1]
    tile = min(64, rows // experts)
    return pl.pallas_call(
        functools.partial(gram_kernel, factor),
        out_shape=jax.ShapeDtypeStruct((rows // experts, experts, width), jnp.bfloat16),
        grid=(rows // experts // tile,),
        in_specs=[
            pl.BlockSpec((tile * experts, depth), lambda i: (i, 0)),
            pl.BlockSpec((depth, width), lambda i: (0, 0)),
        ],
        out_specs=pl.BlockSpec((tile, experts, width), lambda i: (i, 0, 0)),
        compiler_params=pltpu.CompilerParams(vmem_limit_bytes=40 << 20),
        cost_estimate=pl.CostEstimate(
            flops=2 * rows * depth * width,
            bytes_accessed=2 * (rows * depth + depth * width + rows * width),
            transcendentals=0,
        ),
    )(left, right)


def local(tokens, routing, gate_weight, up_weight):
    expert_count = lax.axis_size("expert")
    replica_count = lax.axis_size("dp")
    core = lax.axis_index("dp")
    device_tokens, topk = routing.shape
    local_experts, depth, hidden_width = gate_weight.shape
    factor = 2.0 / (device_tokens * expert_count * replica_count)
    swap = [(0, 1), (1, 0)]

    row_count = -(-device_tokens // ROW_PAD) * ROW_PAD
    extra = ((0, row_count - device_tokens), (0, 0))
    names = jnp.pad(routing, extra, constant_values=-1)
    names = jnp.pad(names, ((0, 0), (0, 128 - topk))).astype(jnp.bfloat16)
    padded = jnp.pad(tokens, extra)
    rows = jnp.stack(
        [
            jnp.concatenate([padded[:, c * depth : (c + 1) * depth], names], axis=1)
            for c in range(replica_count)
        ]
    )
    gathered_rows = gather(rows, expert_count)

    labels = lax.axis_index("expert") * local_experts + jnp.arange(local_experts)

    def gathered(got):
        got = got.reshape(expert_count * row_count, got.shape[-1])
        x = got[:, :depth]
        named = got[:, depth : depth + topk].astype(jnp.int32)
        mask = jnp.any(named[None, :, :] == labels[:, None, None], axis=2)
        return x, mask, lax.ppermute(x[:, :DW], "dp", [(0, 1)])

    own_x, own_mask, sent_own = gathered(gathered_rows[0])
    other_x, other_mask, sent_other = gathered(gathered_rows[1])
    own_window = jnp.where(core == 0, own_x[:, :DW], sent_other)
    other_window = jnp.where(core == 0, other_x[:, :DW], sent_own)

    def project(x, w):
        return jnp.einsum("td,edh->eth", x, w, preferred_element_type=jnp.float32)

    other_gate = lax.ppermute(project(other_x, gate_weight).astype(jnp.bfloat16), "dp", swap)
    other_up = lax.ppermute(project(other_x, up_weight).astype(jnp.bfloat16), "dp", swap)
    gate = project(own_x, gate_weight) + other_gate.astype(jnp.float32)
    up = project(own_x, up_weight) + other_up.astype(jnp.float32)
    hidden = jnp.where(own_mask[:, :, None], jax.nn.silu(gate) * up, 0.0).astype(jnp.bfloat16)
    other_hidden = lax.ppermute(hidden, "dp", swap)

    window = jnp.concatenate([own_window, other_window], axis=0)
    mask = jnp.concatenate([own_mask, other_mask], axis=1)
    block = DW // replica_count
    rows = lax.dynamic_slice_in_dim(window, core * block, block, 1).T
    left = jnp.where(
        jnp.tile(mask, (block, 1)), jnp.repeat(rows, local_experts, axis=0), jnp.bfloat16(0)
    )
    input_gram = gram(left, window, local_experts, factor)

    hidden_all = jnp.concatenate([hidden, other_hidden], axis=1)
    h_block = hidden_width // replica_count
    h_rows = lax.dynamic_slice_in_dim(hidden_all, core * h_block, h_block, 2)
    hidden_gram = jnp.einsum("eti,etj->iej", h_rows, hidden_all, preferred_element_type=jnp.float32)
    return (input_gram, (hidden_gram * factor).astype(jnp.bfloat16))


def solution(mesh):
    placed = (
        P(("groups", "expert", "dp"), None),
        P(("groups", "expert", "dp"), None),
        P("expert", "dp", None),
        P("expert", "dp", None),
    )
    return jax.shard_map(
        local,
        mesh=mesh,
        in_specs=placed,
        out_specs=(P("dp", ("groups", "expert"), None), P("dp", ("groups", "expert"), None)),
        check_vma=False,
    )
```

```python
import functools

import jax
import jax.numpy as jnp
from jax import lax
from jax.experimental import pallas as pl
from jax.experimental.pallas import tpu as pltpu
from jax.sharding import PartitionSpec as P

DW = 2048
ROW_PAD = 16
MESH = pl.DeviceIdType.MESH


def gather_kernel(experts, cores, rows_ref, out_ref, swap_sem, send_sem, recv_sem, own_sem):
    expert, core = lax.axis_index("expert"), lax.axis_index("dp")
    other = {"dp": 1 - core}

    def index_at(place):
        place = lax.rem(place + 2 * experts, experts)
        return jnp.where(2 * place < experts, 2 * place, 2 * (experts - 1 - place) + 1)

    half = expert // 2
    me = jnp.where(lax.rem(expert, 2) == 0, half, experts - 1 - half)
    ways = (1, -1)

    barrier = pltpu.get_barrier_semaphore()
    for way in ways:
        pl.semaphore_signal(
            barrier, inc=1, device_id={"expert": index_at(me + way)}, device_id_type=MESH
        )
    pl.semaphore_signal(barrier, inc=1, device_id=other, device_id_type=MESH)
    pl.semaphore_wait(barrier, 3)

    swap = pltpu.make_async_remote_copy(
        src_ref=rows_ref.at[1 - core],
        dst_ref=out_ref.at[1, expert],
        send_sem=swap_sem.at[0],
        recv_sem=swap_sem.at[1],
        device_id=other,
        device_id_type=MESH,
    )
    swap.start()
    own = pltpu.make_async_copy(rows_ref.at[core], out_ref.at[0, expert], own_sem)
    own.start()

    most = experts // 2
    started = {}
    for hop in range(most):
        for slot in range(cores):
            if hop == 0 and slot == 1:
                swap.wait_recv()
            for side, way in enumerate(ways):
                hops = most if side == slot else experts - 1 - most
                if hop >= hops:
                    continue
                if hop > 0:
                    started[slot, side, hop - 1].wait_recv()
                block = out_ref.at[slot, index_at(me - way * hop)]
                copy = pltpu.make_async_remote_copy(
                    src_ref=rows_ref.at[core] if hop == 0 and slot == 0 else block,
                    dst_ref=block,
                    send_sem=send_sem.at[slot, side, hop],
                    recv_sem=recv_sem.at[slot, side, hop],
                    device_id={"expert": index_at(me + way)},
                    device_id_type=MESH,
                )
                copy.start()
                started[slot, side, hop] = copy
    own.wait()
    swap.wait_send()
    for (slot, side, hop), copy in started.items():
        copy.wait_send()
        if (slot, side, hop + 1) not in started:
            copy.wait_recv()


def gather(rows, experts):
    cores = rows.shape[0]
    steps = (cores, 2, experts // 2)
    return pl.pallas_call(
        functools.partial(gather_kernel, experts, cores),
        out_shape=jax.ShapeDtypeStruct((cores, experts) + rows.shape[1:], rows.dtype),
        in_specs=[pl.BlockSpec(memory_space=pl.ANY)],
        out_specs=pl.BlockSpec(memory_space=pl.ANY),
        scratch_shapes=[
            pltpu.SemaphoreType.DMA((2,)),
            pltpu.SemaphoreType.DMA(steps),
            pltpu.SemaphoreType.DMA(steps),
            pltpu.SemaphoreType.DMA,
        ],
        compiler_params=pltpu.CompilerParams(collective_id=0, has_side_effects=True),
    )(rows)


def gram_kernel(factor, rows_ref, mask_ref, right_ref, out_ref):
    tile, experts, _ = out_ref.shape
    left = rows_ref[...].astype(jnp.float32)[:, None, :] * mask_ref[...][None, :, :]
    left = left.reshape(tile * experts, rows_ref.shape[1]).astype(jnp.bfloat16)
    total = jnp.dot(left, right_ref[...], preferred_element_type=jnp.float32)
    out_ref[...] = (total * factor).reshape(out_ref.shape).astype(out_ref.dtype)


def gram(rows, mask, right, factor):
    count, depth = rows.shape
    experts = mask.shape[0]
    width = right.shape[1]
    tile = 64
    return pl.pallas_call(
        functools.partial(gram_kernel, factor),
        out_shape=jax.ShapeDtypeStruct((count, experts, width), jnp.bfloat16),
        grid=(count // tile,),
        in_specs=[
            pl.BlockSpec((tile, depth), lambda i: (i, 0)),
            pl.BlockSpec((experts, depth), lambda i: (0, 0)),
            pl.BlockSpec((depth, width), lambda i: (0, 0)),
        ],
        out_specs=pl.BlockSpec((tile, experts, width), lambda i: (i, 0, 0)),
        compiler_params=pltpu.CompilerParams(vmem_limit_bytes=40 << 20),
        cost_estimate=pl.CostEstimate(
            flops=2 * count * experts * depth * width,
            bytes_accessed=2 * (count * depth + depth * width + count * experts * width),
            transcendentals=0,
        ),
    )(rows, mask, right)


def local(tokens, routing, gate_weight, up_weight):
    expert_count = lax.axis_size("expert")
    replica_count = lax.axis_size("dp")
    core = lax.axis_index("dp")
    device_tokens, topk = routing.shape
    local_experts, depth, hidden_width = gate_weight.shape
    factor = 2.0 / (device_tokens * expert_count * replica_count)
    swap = [(0, 1), (1, 0)]

    row_count = -(-device_tokens // ROW_PAD) * ROW_PAD
    extra = ((0, row_count - device_tokens), (0, 0))
    names = jnp.pad(routing, extra, constant_values=-1)
    names = jnp.pad(names, ((0, 0), (0, 128 - topk))).astype(jnp.bfloat16)
    padded = jnp.pad(tokens, extra)
    rows = jnp.stack(
        [
            jnp.concatenate([padded[:, c * depth : (c + 1) * depth], names], axis=1)
            for c in range(replica_count)
        ]
    )
    gathered_rows = gather(rows, expert_count)

    labels = lax.axis_index("expert") * local_experts + jnp.arange(local_experts)

    def gathered(got):
        got = got.reshape(expert_count * row_count, got.shape[-1])
        x = got[:, :depth]
        named = got[:, depth : depth + topk].astype(jnp.int32)
        mask = jnp.any(named[None, :, :] == labels[:, None, None], axis=2)
        return x, mask, lax.ppermute(x[:, :DW], "dp", [(0, 1)])

    own_x, own_mask, sent_own = gathered(gathered_rows[0])
    other_x, other_mask, sent_other = gathered(gathered_rows[1])
    own_window = jnp.where(core == 0, own_x[:, :DW], sent_other)
    other_window = jnp.where(core == 0, other_x[:, :DW], sent_own)

    def project(x, w):
        return jnp.einsum("td,edh->eth", x, w, preferred_element_type=jnp.float32)

    other_gate = lax.ppermute(project(other_x, gate_weight).astype(jnp.bfloat16), "dp", swap)
    other_up = lax.ppermute(project(other_x, up_weight).astype(jnp.bfloat16), "dp", swap)
    gate = project(own_x, gate_weight) + other_gate.astype(jnp.float32)
    up = project(own_x, up_weight) + other_up.astype(jnp.float32)
    hidden = jnp.where(own_mask[:, :, None], jax.nn.silu(gate) * up, 0.0).astype(jnp.bfloat16)
    other_hidden = lax.ppermute(hidden, "dp", swap)

    window = jnp.concatenate([own_window, other_window], axis=0)
    mask = jnp.concatenate([own_mask, other_mask], axis=1)
    block = DW // replica_count
    rows = lax.dynamic_slice_in_dim(window, core * block, block, 1).T
    input_gram = gram(rows, mask.astype(jnp.float32), window, factor)

    hidden_all = jnp.concatenate([hidden, other_hidden], axis=1)
    h_block = hidden_width // replica_count
    h_rows = lax.dynamic_slice_in_dim(hidden_all, core * h_block, h_block, 2)
    hidden_gram = jnp.einsum("eti,etj->iej", h_rows, hidden_all, preferred_element_type=jnp.float32)
    return (input_gram, (hidden_gram * factor).astype(jnp.bfloat16))


def solution(mesh):
    placed = (
        P(("groups", "expert", "dp"), None),
        P(("groups", "expert", "dp"), None),
        P("expert", "dp", None),
        P("expert", "dp", None),
    )
    return jax.shard_map(
        local,
        mesh=mesh,
        in_specs=placed,
        out_specs=(P("dp", ("groups", "expert"), None), P("dp", ("groups", "expert"), None)),
        check_vma=False,
    )
```

```python
import functools

import jax
import jax.numpy as jnp
from jax import lax
from jax.experimental import pallas as pl
from jax.experimental.pallas import tpu as pltpu
from jax.sharding import PartitionSpec as P

DW = 2048
ROW_PAD = 16
MESH = pl.DeviceIdType.MESH


def gather_kernel(experts, cores, rows_ref, out_ref, twin_ref, swap_sem, send_sem, recv_sem, own_sem, twin_sem):
    expert, core = lax.axis_index("expert"), lax.axis_index("dp")
    other = {"dp": 1 - core}

    def index_at(place):
        place = lax.rem(place + 2 * experts, experts)
        return jnp.where(2 * place < experts, 2 * place, 2 * (experts - 1 - place) + 1)

    half = expert // 2
    me = jnp.where(lax.rem(expert, 2) == 0, half, experts - 1 - half)
    ways = (1, -1)

    barrier = pltpu.get_barrier_semaphore()
    for way in ways:
        pl.semaphore_signal(
            barrier, inc=1, device_id={"expert": index_at(me + way)}, device_id_type=MESH
        )
    pl.semaphore_signal(barrier, inc=1, device_id=other, device_id_type=MESH)
    pl.semaphore_wait(barrier, 3)

    swap = pltpu.make_async_remote_copy(
        src_ref=rows_ref.at[1 - core],
        dst_ref=out_ref.at[1, expert],
        send_sem=swap_sem.at[0],
        recv_sem=swap_sem.at[1],
        device_id=other,
        device_id_type=MESH,
    )
    swap.start()
    own = pltpu.make_async_copy(rows_ref.at[core], out_ref.at[0, expert], own_sem)
    own.start()

    twins = []

    def hand_over(slot, index):
        twin = pltpu.make_async_remote_copy(
            src_ref=out_ref.at[slot, index],
            dst_ref=twin_ref.at[1 - slot, index],
            send_sem=twin_sem.at[0, len(twins)],
            recv_sem=twin_sem.at[1, len(twins)],
            device_id=other,
            device_id_type=MESH,
        )
        twin.start()
        twins.append(twin)

    most = experts // 2
    started = {}
    for hop in range(most):
        for slot in range(cores):
            if hop == 0 and slot == 1:
                swap.wait_recv()
            for side, way in enumerate(ways):
                hops = most if side == slot else experts - 1 - most
                if hop >= hops:
                    continue
                if hop > 0:
                    started[slot, side, hop - 1].wait_recv()
                    hand_over(slot, index_at(me - way * hop))
                block = out_ref.at[slot, index_at(me - way * hop)]
                copy = pltpu.make_async_remote_copy(
                    src_ref=rows_ref.at[core] if hop == 0 and slot == 0 else block,
                    dst_ref=block,
                    send_sem=send_sem.at[slot, side, hop],
                    recv_sem=recv_sem.at[slot, side, hop],
                    device_id={"expert": index_at(me + way)},
                    device_id_type=MESH,
                )
                copy.start()
                started[slot, side, hop] = copy
    own.wait()
    hand_over(0, expert)
    hand_over(1, expert)
    swap.wait_send()
    for (slot, side, hop), copy in started.items():
        copy.wait_send()
        if (slot, side, hop + 1) not in started:
            copy.wait_recv()
            hand_over(slot, index_at(me - ways[side] * (hop + 1)))
    for twin in twins:
        twin.wait()


def gather(rows, experts):
    cores = rows.shape[0]
    steps = (cores, 2, experts // 2)
    return pl.pallas_call(
        functools.partial(gather_kernel, experts, cores),
        out_shape=[jax.ShapeDtypeStruct((cores, experts) + rows.shape[1:], rows.dtype)] * 2,
        in_specs=[pl.BlockSpec(memory_space=pl.ANY)],
        out_specs=[pl.BlockSpec(memory_space=pl.ANY)] * 2,
        scratch_shapes=[
            pltpu.SemaphoreType.DMA((2,)),
            pltpu.SemaphoreType.DMA(steps),
            pltpu.SemaphoreType.DMA(steps),
            pltpu.SemaphoreType.DMA,
            pltpu.SemaphoreType.DMA((2, cores * experts)),
        ],
        compiler_params=pltpu.CompilerParams(collective_id=0, has_side_effects=True),
    )(rows)


def gram_kernel(factor, rows_ref, mask_ref, right_ref, out_ref):
    tile, experts, _ = out_ref.shape
    left = rows_ref[...].astype(jnp.float32)[:, None, :] * mask_ref[...][None, :, :]
    left = left.reshape(tile * experts, rows_ref.shape[1]).astype(jnp.bfloat16)
    total = jnp.dot(left, right_ref[...], preferred_element_type=jnp.float32)
    out_ref[...] = (total * factor).reshape(out_ref.shape).astype(out_ref.dtype)


def gram(rows, mask, right, factor):
    count, depth = rows.shape
    experts = mask.shape[0]
    width = right.shape[1]
    tile = 64
    return pl.pallas_call(
        functools.partial(gram_kernel, factor),
        out_shape=jax.ShapeDtypeStruct((count, experts, width), jnp.bfloat16),
        grid=(count // tile,),
        in_specs=[
            pl.BlockSpec((tile, depth), lambda i: (i, 0)),
            pl.BlockSpec((experts, depth), lambda i: (0, 0)),
            pl.BlockSpec((depth, width), lambda i: (0, 0)),
        ],
        out_specs=pl.BlockSpec((tile, experts, width), lambda i: (i, 0, 0)),
        compiler_params=pltpu.CompilerParams(vmem_limit_bytes=40 << 20),
        cost_estimate=pl.CostEstimate(
            flops=2 * count * experts * depth * width,
            bytes_accessed=2 * (count * depth + depth * width + count * experts * width),
            transcendentals=0,
        ),
    )(rows, mask, right)


def local(tokens, routing, gate_weight, up_weight):
    expert_count = lax.axis_size("expert")
    replica_count = lax.axis_size("dp")
    core = lax.axis_index("dp")
    device_tokens, topk = routing.shape
    local_experts, depth, hidden_width = gate_weight.shape
    factor = 2.0 / (device_tokens * expert_count * replica_count)
    swap = [(0, 1), (1, 0)]

    row_count = -(-device_tokens // ROW_PAD) * ROW_PAD
    extra = ((0, row_count - device_tokens), (0, 0))
    names = jnp.pad(routing, extra, constant_values=-1)
    names = jnp.pad(names, ((0, 0), (0, 128 - topk))).astype(jnp.bfloat16)
    padded = jnp.pad(tokens, extra)
    rows = jnp.stack(
        [
            jnp.concatenate([padded[:, c * depth : (c + 1) * depth], names], axis=1)
            for c in range(replica_count)
        ]
    )
    gathered_rows, twin_rows = gather(rows, expert_count)

    labels = lax.axis_index("expert") * local_experts + jnp.arange(local_experts)

    def gathered(got, twin):
        got = got.reshape(expert_count * row_count, got.shape[-1])
        twin = twin.reshape(got.shape)
        x = got[:, :depth]
        named = got[:, depth : depth + topk].astype(jnp.int32)
        mask = jnp.any(named[None, :, :] == labels[:, None, None], axis=2)
        return x, mask, jnp.where(core == 0, x[:, :DW], twin[:, :DW])

    own_x, own_mask, own_window = gathered(gathered_rows[0], twin_rows[0])
    other_x, other_mask, other_window = gathered(gathered_rows[1], twin_rows[1])

    def project(x, w):
        return jnp.einsum("td,edh->eth", x, w, preferred_element_type=jnp.float32)

    other_gate = lax.ppermute(project(other_x, gate_weight).astype(jnp.bfloat16), "dp", swap)
    other_up = lax.ppermute(project(other_x, up_weight).astype(jnp.bfloat16), "dp", swap)
    gate = project(own_x, gate_weight) + other_gate.astype(jnp.float32)
    up = project(own_x, up_weight) + other_up.astype(jnp.float32)
    hidden = jnp.where(own_mask[:, :, None], jax.nn.silu(gate) * up, 0.0).astype(jnp.bfloat16)
    other_hidden = lax.ppermute(hidden, "dp", swap)

    window = jnp.concatenate([own_window, other_window], axis=0)
    mask = jnp.concatenate([own_mask, other_mask], axis=1)
    block = DW // replica_count
    rows = lax.dynamic_slice_in_dim(window, core * block, block, 1).T
    input_gram = gram(rows, mask.astype(jnp.float32), window, factor)

    hidden_all = jnp.concatenate([hidden, other_hidden], axis=1)
    h_block = hidden_width // replica_count
    h_rows = lax.dynamic_slice_in_dim(hidden_all, core * h_block, h_block, 2)
    hidden_gram = jnp.einsum("eti,etj->iej", h_rows, hidden_all, preferred_element_type=jnp.float32)
    return (input_gram, (hidden_gram * factor).astype(jnp.bfloat16))


def solution(mesh):
    placed = (
        P(("groups", "expert", "dp"), None),
        P(("groups", "expert", "dp"), None),
        P("expert", "dp", None),
        P("expert", "dp", None),
    )
    return jax.shard_map(
        local,
        mesh=mesh,
        in_specs=placed,
        out_specs=(P("dp", ("groups", "expert"), None), P("dp", ("groups", "expert"), None)),
        check_vma=False,
    )
```
